32 devices in a mesh: ctx: 8 (over z, x), tp: 4 (over y, core).
Axes of the slice: x: 2, y: 2, z: 4, core: 2. Of those that a mesh axis runs over, the one named last changes fastest.
Arguments:
- hidden_in: bfloat16 [4096, 4096], P('ctx', 'tp'), may hold values from -6 to 6
- norm_gain: bfloat16 [1, 4096], P(None, 'ctx'), may hold values from 0.25 to 1.75
- w_qkv: bfloat16 [1, 3, 4096, 512], P(None, None, 'ctx', 'tp'), may hold values from -0.09375 to 0.09375
- w_out: bfloat16 [1, 512, 4096], P(None, 'tp', 'ctx'), may hold values from -1 to 1
Outputs:
- hidden_out: bfloat16 [4096, 4096], P('ctx', 'tp')
The draws below stay inside these ranges and needn't reach their ends.
All inputs are finite; a program needn't handle non-finite values.
Results may differ from the reference program's by a relative error of at most 0.015.
Values may be sent and summed in bfloat16 or wider, within the bound.
A program may use at most 64 MiB of HBM per device.

```python
import math
import jax
import jax.numpy as jnp
from jax import lax

D = 4096
HD = 128
LAYERS = 1
SEG = 512
HEADS = 4
TOKENS = 4096
N_CTX = 8


def shard_levels(rng, dims, split, least, high):
    def one(dim, shards_of):
        steps = jax.random.uniform(jax.random.fold_in(jax.random.fold_in(rng, 6), dim), (shards_of,), jnp.float32, least / len(split), high / len(split))
        return jnp.repeat(jnp.exp(steps), dims[dim] // shards_of).reshape((-1,) + (1,) * (len(dims) - dim - 1))

    factor_of = one(*split[0])
    for cut in split[1:]:
        factor_of = factor_of * one(*cut)
    return factor_of


def scatter_about(stream_key, shape, spread, reach, split=(), held_as=jnp.bfloat16):
    gain = shard_levels(stream_key, shape, split, -0.22, 0.18) if split else 1.0
    values = jax.random.normal(stream_key, shape, jnp.float32) * spread * gain
    return jnp.minimum(jnp.maximum(values, -reach), reach).astype(held_as)


def setup_inputs(seed: int = 0) -> dict:
    streams_of = jax.random.split(jax.random.key(seed), 5)
    hidden_in = scatter_about(streams_of[0], (TOKENS, D), 1.0, 6.0, ((0, 8), (1, 4)))
    norm_gain = jnp.clip(1.0 + 0.15 * jax.random.normal(streams_of[1], (LAYERS, D), jnp.float32), 0.25, 1.75).astype(jnp.bfloat16)
    w_qkv = scatter_about(streams_of[2], (LAYERS, 3, D, HEADS * HD), D ** -0.5, 0.09375, ((2, 8), (3, 4)))
    w_out = scatter_about(streams_of[3], (LAYERS, HEADS * HD, D), (HD // 4) ** -0.5, 1.0, ((1, 4), (2, 8)))
    return dict(hidden_in=hidden_in, norm_gain=norm_gain, w_qkv=w_qkv, w_out=w_out)


def normalize(hidden):
    values = hidden.astype(jnp.float32)
    return values * lax.rsqrt(lax.optimization_barrier(jnp.mean(values * values, axis=-1, keepdims=True)) + 1e-06)

def round_trip(values):
    return lax.optimization_barrier(values.astype(jnp.bfloat16)).astype(jnp.float32)

def attend(queries, key_rows, value_rows):
    heads = queries.shape[1] // HD
    shaped_q = queries.reshape(N_CTX, SEG, heads, HD)
    shaped_k = key_rows.reshape(N_CTX, SEG, heads, HD)
    shaped_v = value_rows.reshape(N_CTX, SEG, heads, HD)
    blank_seg = jnp.zeros((1, SEG, heads, HD), shaped_k.dtype)
    prev_k = jnp.concatenate([blank_seg, shaped_k[:-1]], axis=0)
    prev_v = jnp.concatenate([blank_seg, shaped_v[:-1]], axis=0)
    score_scale = 1.0 / math.sqrt(HD)
    row_ids = jnp.arange(SEG)[:, None]
    col_ids = jnp.arange(2 * SEG)[None, :]
    own_allowed = (col_ids >= SEG) & (col_ids - SEG <= row_ids)

    def one_segment(items):
        seg_q, seg_pk, seg_k, seg_pv, seg_v, seg_id = items
        keys_all = jnp.concatenate([seg_pk, seg_k], axis=0).astype(jnp.float32)
        values_all = jnp.concatenate([seg_pv, seg_v], axis=0).astype(jnp.float32)
        scores = jnp.einsum('qhd,khd->hqk', seg_q.astype(jnp.float32), keys_all) * score_scale
        allowed = own_allowed | (col_ids < SEG) & (seg_id > 0)
        exp_scores = jnp.where(allowed[None], jnp.exp(scores), 0.0)
        probs = round_trip(exp_scores / lax.optimization_barrier(jnp.sum(exp_scores, axis=-1, keepdims=True)))
        return jnp.einsum('hqk,khd->qhd', probs, values_all).astype(jnp.bfloat16)
    seg_ids = jnp.arange(N_CTX).astype(jnp.int32)
    attended = lax.map(one_segment, (shaped_q, prev_k, shaped_k, prev_v, shaped_v, seg_ids))
    return attended.reshape(N_CTX * SEG, heads * HD)

def reference(hidden_in, norm_gain, w_qkv, w_out):
    hidden = hidden_in
    for layer_index in range(LAYERS):
        normed = (normalize(hidden) * norm_gain[layer_index].astype(jnp.float32)).astype(jnp.bfloat16)
        queries = jnp.dot(normed, w_qkv[layer_index, 0], preferred_element_type=jnp.float32).astype(jnp.bfloat16)
        key_rows = jnp.dot(normed, w_qkv[layer_index, 1], preferred_element_type=jnp.float32).astype(jnp.bfloat16)
        value_rows = jnp.dot(normed, w_qkv[layer_index, 2], preferred_element_type=jnp.float32).astype(jnp.bfloat16)
        attended = attend(queries, key_rows, value_rows)
        out_weight = w_out[layer_index]

        def add_head(head_index, running):
            head_part = lax.dynamic_slice_in_dim(attended, head_index * HD, HD, 1)
            head_rows = lax.dynamic_slice_in_dim(out_weight, head_index * HD, HD, 0)
            return running + round_trip(jnp.dot(head_part, head_rows, preferred_element_type=jnp.float32))
        branch = lax.fori_loop(0, HEADS, add_head, jnp.zeros((N_CTX * SEG, D), jnp.float32))
        hidden = (hidden.astype(jnp.float32) + branch).astype(jnp.bfloat16)
    return hidden
```

```python
import functools
import math

import jax
import jax.numpy as jnp
from jax import lax
from jax.experimental import pallas as pl
from jax.experimental.pallas import tpu as pltpu
from jax.sharding import PartitionSpec as P

HD = 128
PAIR = 2
HIDDEN_CHUNKS = 2
KINDS = (1, 2, 0)


def kernel(
    n_ctx, n_tp,
    hid_ref, gain_ref, w_ref, o_ref, out_ref,
    hbuf, wbuf, obuf, wouse, kv, mem, qbuf, att, scale,
    w_recv, w_send, ol_recv, ol_send, ot_recv, ot_send, ox_recv, ox_send,
    h_recv, hs_send, hy_send, hf_send, kv_recv, kv_send, a_recv, a_send,
):
    line = n_ctx // PAIR
    n_y = n_tp // 2
    c = lax.axis_index("ctx")
    t = lax.axis_index("tp")
    a = lax.div(c, PAIR)
    b = lax.rem(c, PAIR)
    y = lax.div(t, 2)
    core = lax.rem(t, 2)
    seg, own_d = hid_ref.shape
    depth = w_ref.shape[1]
    rows_c = seg // HIDDEN_CHUNKS
    pair_c = PAIR * a + (1 - b)
    sib = 2 * y + (1 - core)
    has_right = a + 1 < line
    has_left = a >= 1

    def remote(src, dst, send, recv, ctx=None, tp=None):
        where = {}
        if ctx is not None:
            where["ctx"] = ctx
        if tp is not None:
            where["tp"] = tp
        return pltpu.make_async_remote_copy(
            src_ref=src, dst_ref=dst, send_sem=send, recv_sem=recv,
            device_id=where, device_id_type=pl.DeviceIdType.MESH,
        )

    barrier = pltpu.get_barrier_semaphore()

    def greet(**where):
        pl.semaphore_signal(barrier, inc=1, device_id=where, device_id_type=pl.DeviceIdType.MESH)

    greet(ctx=pair_c)
    for p in range(n_tp):
        @pl.when(p != t)
        def _():
            greet(tp=p)

    @pl.when(has_right)
    def _():
        greet(ctx=c + PAIR)

    @pl.when(has_left)
    def _():
        greet(ctx=c - PAIR)

    @pl.when((b == 1) & (c + 1 < n_ctx))
    def _():
        greet(ctx=c + 1)

    @pl.when((b == 0) & (c > 0))
    def _():
        greet(ctx=c - 1)

    gain = jnp.transpose(jnp.broadcast_to(gain_ref[...].astype(jnp.float32), (HD, depth)))
    for kind in KINDS:
        wbuf[kind, c] = (w_ref[kind].astype(jnp.float32) * gain).astype(jnp.bfloat16)
    obuf[a] = o_ref[...]
    hbuf[t] = hid_ref[...]

    @pl.when(c == 0)
    def _():
        mem[...] = jnp.zeros_like(mem)

    total = n_tp + has_right.astype(jnp.int32) + has_left.astype(jnp.int32)
    total += ((b == 1) & (c + 1 < n_ctx)).astype(jnp.int32)
    total += ((b == 0) & (c > 0)).astype(jnp.int32)
    pl.semaphore_wait(barrier, total)

    def h_part(slot, i):
        return hbuf.at[slot, pl.ds(i * rows_c, rows_c), :]

    def h_copy(slot, i, send, dest):
        part = h_part(slot, i)
        return remote(part, part, send, h_recv.at[slot, i], tp=dest)

    for i in range(HIDDEN_CHUNKS):
        for q in range(n_y):
            @pl.when(q != y)
            def _():
                h_copy(t, i, hy_send.at[q, i], 2 * q + core).start()

    def w_copy(kind, pa, way):
        pc = PAIR * pa + b
        slot = wbuf.at[kind, pc]
        dest = (c + PAIR, c - PAIR, pair_c)[way]
        return remote(slot, slot, w_send.at[kind, pa, way], w_recv.at[kind, pc], ctx=dest)

    def o_line(pa, way):
        slot = obuf.at[pa]
        dest = (c + PAIR, c - PAIR)[way]
        return remote(slot, slot, ol_send.at[pa, way], ol_recv.at[pa], ctx=dest)

    def o_tp(pa):
        dst = wouse.at[b, pl.ds(pl.multiple_of(t * HD, HD), HD), :]
        return remote(obuf.at[pa], dst, ot_send.at[pa], ot_recv.at[t], tp=pa)

    def o_pair(head):
        part = wouse.at[b, pl.ds(pl.multiple_of(head * HD, HD), HD), :]
        return remote(part, part, ox_send.at[head], ox_recv.at[head], ctx=pair_c)

    def own_sends(kind):
        @pl.when(has_right)
        def _():
            w_copy(kind, a, 0).start()

        @pl.when(has_left)
        def _():
            w_copy(kind, a, 1).start()

        w_copy(kind, a, 2).start()

    def own_o():
        @pl.when(has_right)
        def _():
            o_line(a, 0).start()

        @pl.when(has_left)
        def _():
            o_line(a, 1).start()

        o_route(a)

    def o_route(pa):
        @pl.when(pa == t)
        def _():
            wouse[b, pl.ds(pl.multiple_of(t * HD, HD), HD), :] = obuf[pa]
            o_pair(t).start()

        @pl.when(pa != t)
        def _():
            o_tp(pa).start()

    def w_wait(kind, pc):
        slot = wbuf.at[kind, pc]
        remote(slot, slot, w_send.at[kind, 0, 0], w_recv.at[kind, pc], ctx=pair_c).wait_recv()

    def pass_on(kind):
        def body(d, carry):
            @pl.when(a - d >= 0)
            def _():
                w_wait(kind, c - PAIR * d)

                @pl.when(has_right)
                def _():
                    w_copy(kind, a - d, 0).start()

                w_copy(kind, a - d, 2).start()

            @pl.when(a + d < line)
            def _():
                w_wait(kind, c + PAIR * d)

                @pl.when(has_left)
                def _():
                    w_copy(kind, a + d, 1).start()

                w_copy(kind, a + d, 2).start()

            return carry

        lax.fori_loop(1, line, body, 0)

    def pass_o():
        def body(d, carry):
            @pl.when(a - d >= 0)
            def _():
                o_line(a - d, 0).wait_recv()

                @pl.when(has_right)
                def _():
                    o_line(a - d, 0).start()

                o_route(a - d)

            @pl.when(a + d < line)
            def _():
                o_line(a + d, 1).wait_recv()

                @pl.when(has_left)
                def _():
                    o_line(a + d, 1).start()

                o_route(a + d)

            return carry

        lax.fori_loop(1, line, body, 0)

    def h_forward(i):
        for q in range(n_y):
            @pl.when(q != y)
            def _():
                slot = 2 * q + core
                h_copy(slot, i, hf_send.at[q, i], sib).wait_recv()
                h_copy(slot, i, hf_send.at[q, i], sib).start()

    def pair_wait(kind):
        def body(pa, carry):
            w_wait(kind, PAIR * pa + (1 - b))
            return carry

        lax.fori_loop(0, line, body, 0)

    own_sends(KINDS[0])
    for i in range(HIDDEN_CHUNKS):
        h_copy(t, i, hs_send.at[i], sib).start()
    own_sends(KINDS[1])
    pass_on(KINDS[0])
    own_sends(KINDS[2])
    pass_on(KINDS[1])
    h_forward(0)
    own_o()
    pass_on(KINDS[2])
    for i in range(1, HIDDEN_CHUNKS):
        h_forward(i)

    for i in range(HIDDEN_CHUNKS):
        h_copy(sib, i, hs_send.at[i], sib).wait_recv()
        for q in range(n_y):
            @pl.when(q != y)
            def _():
                h_copy(2 * q + 1 - core, i, hs_send.at[i], sib).wait_recv()

    def squares(p, sums):
        part = hbuf[p].astype(jnp.float32)
        return sums + jnp.sum(part * part, axis=1, keepdims=True)

    sums = lax.fori_loop(0, n_tp, squares, jnp.zeros((seg, 1), jnp.float32))
    scale[...] = jnp.broadcast_to(
        lax.rsqrt(sums / (own_d * n_tp) + 1e-06), scale.shape
    )

    def project(kinds):
        width = HD * len(kinds)

        def body(p, acc):
            w = [
                wbuf[k, pl.ds(PAIR * p, PAIR)].reshape(PAIR * depth, HD) for k in kinds
            ]
            w = w[0] if len(w) == 1 else jnp.concatenate(w, axis=1)
            return acc + jnp.dot(hbuf[p], w, preferred_element_type=jnp.float32)

        return lax.fori_loop(0, n_tp, body, jnp.zeros((seg, width), jnp.float32))

    pair_wait(1)
    pair_wait(2)
    proj = project((1, 2))
    kv[0] = (proj[:, :HD] * scale[...]).astype(jnp.bfloat16)
    kv[1] = (proj[:, HD:] * scale[...]).astype(jnp.bfloat16)

    def kv_copy(dest):
        return remote(kv, mem, kv_send, kv_recv, ctx=dest)

    @pl.when(c + 1 < n_ctx)
    def _():
        kv_copy(c + 1).start()

    pass_o()
    for p in range(n_tp):
        @pl.when(p != t)
        def _():
            part = wouse.at[b, pl.ds(p * HD, HD), :]
            remote(part, part, ot_send.at[0], ot_recv.at[p], tp=p).wait_recv()
            o_pair(p).start()

    pair_wait(0)
    qbuf[...] = (project((0,)) * scale[...] * (1.0 / math.sqrt(HD))).astype(jnp.bfloat16)

    @pl.when(c > 0)
    def _():
        kv_copy(c).wait_recv()

    q_rows = min(128, seg)
    mine = pl.ds(pl.multiple_of(t * HD, HD), HD)

    def attend(i, carry):
        rows = pl.ds(pl.multiple_of(i * q_rows, q_rows), q_rows)
        q = qbuf[rows, :]
        nt = (((1,), (1,)), ((), ()))
        s_mem = lax.dot_general(q, mem[0], nt, preferred_element_type=jnp.float32)
        s_own = lax.dot_general(q, kv[0], nt, preferred_element_type=jnp.float32)
        s_mem = jnp.where(c > 0, s_mem, -1e30)
        row = lax.broadcasted_iota(jnp.int32, s_own.shape, 0) + i * q_rows
        col = lax.broadcasted_iota(jnp.int32, s_own.shape, 1)
        s_own = jnp.where(col <= row, s_own, -1e30)
        top = jnp.maximum(
            jnp.max(s_mem, axis=1, keepdims=True), jnp.max(s_own, axis=1, keepdims=True)
        )
        e_mem = jnp.exp(s_mem - top)
        e_own = jnp.exp(s_own - top)
        total = jnp.sum(e_mem, axis=1, keepdims=True) + jnp.sum(e_own, axis=1, keepdims=True)
        mixed = jnp.dot(e_mem.astype(jnp.bfloat16), mem[1], preferred_element_type=jnp.float32)
        mixed += jnp.dot(e_own.astype(jnp.bfloat16), kv[1], preferred_element_type=jnp.float32)
        att[rows, mine] = (mixed / total).astype(jnp.bfloat16)
        return carry

    lax.fori_loop(0, seg // q_rows, attend, 0)

    def att_copy(head, dest):
        part = att.at[:, pl.ds(pl.multiple_of(head * HD, HD), HD)]
        return remote(part, part, a_send.at[dest], a_recv.at[head], tp=dest)

    for p in range(n_tp):
        @pl.when(p != t)
        def _():
            att_copy(t, p).start()

    for p in range(n_tp):
        @pl.when(p != t)
        def _():
            att_copy(p, p).wait_recv()
    for p in range(n_tp):
        part = wouse.at[1 - b, pl.ds(p * HD, HD), :]
        remote(part, part, ox_send.at[p], ox_recv.at[p], ctx=pair_c).wait_recv()

    wide = o_ref.shape[1]
    o_rows = min(128, seg)

    def final(i, carry):
        rows = pl.ds(pl.multiple_of(i * o_rows, o_rows), o_rows)
        for r in range(PAIR):
            cols = pl.ds(r * wide, wide)
            branch = jnp.dot(att[rows, :], wouse[r], preferred_element_type=jnp.float32)
            out_ref[rows, cols] = (hid_ref[rows, cols].astype(jnp.float32) + branch).astype(
                out_ref.dtype
            )
        return carry

    lax.fori_loop(0, seg // o_rows, final, 0)

    for i in range(HIDDEN_CHUNKS):
        h_copy(t, i, hs_send.at[i], sib).wait_send()
        for q in range(n_y):
            @pl.when(q != y)
            def _():
                h_copy(t, i, hy_send.at[q, i], 2 * q + core).wait_send()
                h_copy(2 * q + core, i, hf_send.at[q, i], sib).wait_send()

    def drain(pa, carry):
        right = has_right & (pa <= a)
        left = has_left & (pa >= a)
        for kind in KINDS:
            w_copy(kind, pa, 2).wait_send()

        @pl.when(right)
        def _():
            for kind in KINDS:
                w_copy(kind, pa, 0).wait_send()
            o_line(pa, 0).wait_send()

        @pl.when(left)
        def _():
            for kind in KINDS:
                w_copy(kind, pa, 1).wait_send()
            o_line(pa, 1).wait_send()

        @pl.when(pa != t)
        def _():
            o_tp(pa).wait_send()

        return carry

    lax.fori_loop(0, line, drain, 0)
    for p in range(n_tp):
        o_pair(p).wait_send()

        @pl.when(p != t)
        def _():
            att_copy(t, p).wait_send()

    @pl.when(c + 1 < n_ctx)
    def _():
        kv_copy(c + 1).wait_send()


def per_device(n_ctx, n_tp, hidden, norm_gain, w_qkv, w_out):
    seg, own_d = hidden.shape
    _, kinds, depth, head = w_qkv.shape
    wide = w_out.shape[2]
    line, n_y = n_ctx // PAIR, n_tp // 2
    bf16, f32 = jnp.bfloat16, jnp.float32
    dma = pltpu.SemaphoreType.DMA
    vmem = pl.BlockSpec(memory_space=pltpu.VMEM)
    flops = 2 * seg * own_d * n_tp * 3 * HD + 8 * seg * seg * HD + 2 * seg * HD * n_tp * own_d
    return pl.pallas_call(
        functools.partial(kernel, n_ctx, n_tp),
        out_shape=jax.ShapeDtypeStruct((seg, own_d), hidden.dtype),
        in_specs=[vmem] * 4,
        out_specs=vmem,
        scratch_shapes=[
            pltpu.VMEM((n_tp, seg, own_d), bf16),
            pltpu.VMEM((kinds, n_ctx, depth, head), bf16),
            pltpu.VMEM((line, head, wide), bf16),
            pltpu.VMEM((PAIR, n_tp * head, wide), bf16),
            pltpu.VMEM((2, seg, head), bf16),
            pltpu.VMEM((2, seg, head), bf16),
            pltpu.VMEM((seg, head), bf16),
            pltpu.VMEM((seg, n_tp * head), bf16),
            pltpu.VMEM((seg, head), f32),
            dma((kinds, n_ctx)),
            dma((kinds, line, 3)),
            dma((line,)),
            dma((line, 2)),
            dma((n_tp,)),
            dma((line,)),
            dma((n_tp,)),
            dma((n_tp,)),
            dma((n_tp, HIDDEN_CHUNKS)),
            dma((HIDDEN_CHUNKS,)),
            dma((n_y, HIDDEN_CHUNKS)),
            dma((n_y, HIDDEN_CHUNKS)),
            dma,
            dma,
            dma((n_tp,)),
            dma((n_tp,)),
        ],
        compiler_params=pltpu.CompilerParams(
            collective_id=0, has_side_effects=True, vmem_limit_bytes=48 * 1024 * 1024
        ),
        cost_estimate=pl.CostEstimate(
            flops=flops, bytes_accessed=4 * seg * own_d, transcendentals=2 * seg * seg
        ),
    )(hidden, norm_gain, w_qkv[0], w_out[0])


def solution(mesh):
    n_ctx, n_tp = mesh.shape["ctx"], mesh.shape["tp"]
    placed = (P("ctx", "tp"), P(None, "ctx"), P(None, None, "ctx", "tp"), P(None, "tp", "ctx"))
    return jax.shard_map(
        functools.partial(per_device, n_ctx, n_tp),
        mesh=mesh, in_specs=placed, out_specs=P("ctx", "tp"), check_vma=False,
    )
```

```python
import functools
import math

import jax
import jax.numpy as jnp
from jax import lax
from jax.experimental import pallas as pl
from jax.experimental.pallas import tpu as pltpu
from jax.sharding import PartitionSpec as P

HD = 128
PAIR = 2
HIDDEN_CHUNKS = 2
ATT_CHUNKS = 2
KINDS = (1, 2, 0)


def kernel(
    n_ctx, n_tp,
    hid_ref, gain_ref, w_ref, o_ref, out_ref,
    wstage, gstage, ostage, hbuf, wbuf, obuf, wouse, kv, mem, qbuf, att, scale,
    w_recv, w_send, ol_recv, ol_send, ot_recv, ot_send, ox_recv, ox_send,
    h_recv, hs_send, hy_send, hf_send, kv_recv, kv_send, a_recv, a_send, in_sem, out_sem,
):
    line = n_ctx // PAIR
    n_y = n_tp // 2
    c = lax.axis_index("ctx")
    t = lax.axis_index("tp")
    a = lax.div(c, PAIR)
    b = lax.rem(c, PAIR)
    y = lax.div(t, 2)
    core = lax.rem(t, 2)
    seg, own_d = hid_ref.shape
    depth = w_ref.shape[2]
    rows_c = seg // HIDDEN_CHUNKS
    pair_c = PAIR * a + (1 - b)
    sib = 2 * y + (1 - core)
    has_right = a + 1 < line
    has_left = a >= 1

    def remote(src, dst, send, recv, ctx=None, tp=None):
        where = {}
        if ctx is not None:
            where["ctx"] = ctx
        if tp is not None:
            where["tp"] = tp
        return pltpu.make_async_remote_copy(
            src_ref=src, dst_ref=dst, send_sem=send, recv_sem=recv,
            device_id=where, device_id_type=pl.DeviceIdType.MESH,
        )

    loads = [
        pltpu.make_async_copy(gain_ref, gstage, in_sem.at[0]),
        pltpu.make_async_copy(w_ref.at[0], wstage, in_sem.at[1]),
        pltpu.make_async_copy(hid_ref, hbuf.at[t], in_sem.at[2]),
        pltpu.make_async_copy(o_ref.at[0], obuf.at[a], in_sem.at[3]),
    ]
    for load in loads:
        load.start()

    barrier = pltpu.get_barrier_semaphore()

    def greet(**where):
        pl.semaphore_signal(barrier, inc=1, device_id=where, device_id_type=pl.DeviceIdType.MESH)

    greet(ctx=pair_c)
    for p in range(n_tp):
        @pl.when(p != t)
        def _():
            greet(tp=p)

    @pl.when(has_right)
    def _():
        greet(ctx=c + PAIR)

    @pl.when(has_left)
    def _():
        greet(ctx=c - PAIR)

    @pl.when((b == 1) & (c + 1 < n_ctx))
    def _():
        greet(ctx=c + 1)

    @pl.when((b == 0) & (c > 0))
    def _():
        greet(ctx=c - 1)

    loads[0].wait()
    loads[1].wait()
    gain = jnp.transpose(jnp.broadcast_to(gstage[...].astype(jnp.float32), (HD, depth)))
    for kind in KINDS:
        wbuf[kind, c] = (wstage[kind].astype(jnp.float32) * gain).astype(jnp.bfloat16)
    loads[2].wait()
    loads[3].wait()

    @pl.when(c == 0)
    def _():
        mem[...] = jnp.zeros_like(mem)

    total = n_tp + has_right.astype(jnp.int32) + has_left.astype(jnp.int32)
    total += ((b == 1) & (c + 1 < n_ctx)).astype(jnp.int32)
    total += ((b == 0) & (c > 0)).astype(jnp.int32)
    pl.semaphore_wait(barrier, total)

    def h_part(slot, i):
        return hbuf.at[slot, pl.ds(i * rows_c, rows_c), :]

    def h_copy(slot, i, send, dest):
        part = h_part(slot, i)
        return remote(part, part, send, h_recv.at[slot, i], tp=dest)

    for i in range(HIDDEN_CHUNKS):
        for q in range(n_y):
            @pl.when(q != y)
            def _():
                h_copy(t, i, hy_send.at[q, i], 2 * q + core).start()

    def w_copy(kind, pc, way):
        slot = wbuf.at[kind, pc]
        dest = (c + PAIR, c - PAIR, pair_c)[way]
        return remote(slot, slot, w_send.at[kind, pc, way], w_recv.at[kind, pc], ctx=dest)

    def o_line(pa, way):
        slot = obuf.at[pa]
        dest = (c + PAIR, c - PAIR)[way]
        return remote(slot, slot, ol_send.at[pa, way], ol_recv.at[pa], ctx=dest)

    def o_tp(pa):
        dst = wouse.at[b, pl.ds(pl.multiple_of(t * HD, HD), HD), :]
        return remote(obuf.at[pa], dst, ot_send.at[pa], ot_recv.at[t], tp=pa)

    def o_pair(head):
        part = wouse.at[b, pl.ds(pl.multiple_of(head * HD, HD), HD), :]
        return remote(part, part, ox_send.at[head], ox_recv.at[head], ctx=pair_c)

    def line_sends(kind, pc):
        @pl.when(has_right)
        def _():
            w_copy(kind, pc, 0).start()

        @pl.when(has_left)
        def _():
            w_copy(kind, pc, 1).start()

    def own_o():
        @pl.when(has_right)
        def _():
            o_line(a, 0).start()

        @pl.when(has_left)
        def _():
            o_line(a, 1).start()

        o_route(a)

    def o_route(pa):
        @pl.when(pa == t)
        def _():
            wouse[b, pl.ds(pl.multiple_of(t * HD, HD), HD), :] = obuf[pa]
            o_pair(t).start()

        @pl.when(pa != t)
        def _():
            o_tp(pa).start()

    def w_wait(kind, pc):
        w_copy(kind, pc, 2).wait_recv()

    def pass_on(kind, first, last):
        both = kind == KINDS[-1]
        parities = (b, 1 - b) if both else (b,)

        def body(d, carry):
            for parity in parities:
                @pl.when(a - d >= 0)
                def _():
                    pc = PAIR * (a - d) + parity
                    w_wait(kind, pc)

                    @pl.when(has_right)
                    def _():
                        w_copy(kind, pc, 0).start()

                    if not both:
                        w_copy(kind, pc, 2).start()

                @pl.when(a + d < line)
                def _():
                    pc = PAIR * (a + d) + parity
                    w_wait(kind, pc)

                    @pl.when(has_left)
                    def _():
                        w_copy(kind, pc, 1).start()

                    if not both:
                        w_copy(kind, pc, 2).start()

            return carry

        lax.fori_loop(first, last, body, 0)

    def o_forward(d):
        @pl.when((a - t == d) | (t - a == d))
        def _():
            def one(p, carry):
                @pl.when(p != t)
                def _():
                    part = wouse.at[b, pl.ds(pl.multiple_of(p * HD, HD), HD), :]
                    remote(part, part, ot_send.at[0], ot_recv.at[p], tp=p).wait_recv()
                    o_pair(p).start()

                return carry

            lax.fori_loop(0, n_tp, one, 0)

    def pass_o(first, last):
        def body(d, carry):
            @pl.when(a - d >= 0)
            def _():
                o_line(a - d, 0).wait_recv()

                @pl.when(has_right)
                def _():
                    o_line(a - d, 0).start()

                o_route(a - d)

            @pl.when(a + d < line)
            def _():
                o_line(a + d, 1).wait_recv()

                @pl.when(has_left)
                def _():
                    o_line(a + d, 1).start()

                o_route(a + d)

            o_forward(d - 1)
            return carry

        lax.fori_loop(first, last, body, 0)

    def h_forward(i):
        for q in range(n_y):
            @pl.when(q != y)
            def _():
                slot = 2 * q + core
                h_copy(slot, i, hf_send.at[q, i], sib).wait_recv()
                h_copy(slot, i, hf_send.at[q, i], sib).start()

    def pair_wait(kind):
        def body(pa, carry):
            w_wait(kind, PAIR * pa + (1 - b))
            return carry

        lax.fori_loop(0, line, body, 0)

    kind_k, kind_v, kind_q = KINDS
    line_sends(kind_k, c)
    w_copy(kind_k, c, 2).start()
    w_copy(kind_q, c, 2).start()
    for i in range(HIDDEN_CHUNKS):
        h_copy(t, i, hs_send.at[i], sib).start()
    line_sends(kind_v, c)
    w_copy(kind_v, c, 2).start()
    pass_on(kind_k, 1, line)
    line_sends(kind_q, c)
    w_wait(kind_q, pair_c)
    line_sends(kind_q, pair_c)
    pass_on(kind_v, 1, line)
    h_forward(0)
    own_o()
    pass_on(kind_q, 1, line - 1)
    for i in range(1, HIDDEN_CHUNKS):
        h_forward(i)

    for i in range(HIDDEN_CHUNKS):
        h_copy(sib, i, hs_send.at[i], sib).wait_recv()
        for q in range(n_y):
            @pl.when(q != y)
            def _():
                h_copy(2 * q + 1 - core, i, hs_send.at[i], sib).wait_recv()

    def squares(p, sums):
        part = hbuf[p].astype(jnp.float32)
        return sums + jnp.sum(part * part, axis=1, keepdims=True)

    sums = lax.fori_loop(0, n_tp, squares, jnp.zeros((seg, 1), jnp.float32))
    scale[...] = jnp.broadcast_to(
        lax.rsqrt(sums / (own_d * n_tp) + 1e-06), scale.shape
    )

    def project(kinds):
        width = HD * len(kinds)

        def body(p, acc):
            w = [
                wbuf[k, pl.ds(PAIR * p, PAIR)].reshape(PAIR * depth, HD) for k in kinds
            ]
            w = w[0] if len(w) == 1 else jnp.concatenate(w, axis=1)
            return acc + jnp.dot(hbuf[p], w, preferred_element_type=jnp.float32)

        return lax.fori_loop(0, n_tp, body, jnp.zeros((seg, width), jnp.float32))

    pair_wait(1)
    pair_wait(2)
    proj = project((1, 2))
    kv[0] = (proj[:, :HD] * scale[...]).astype(jnp.bfloat16)
    kv[1] = (proj[:, HD:] * scale[...]).astype(jnp.bfloat16)

    def kv_copy(dest):
        return remote(kv, mem, kv_send, kv_recv, ctx=dest)

    @pl.when(c + 1 < n_ctx)
    def _():
        kv_copy(c + 1).start()

    pass_on(kind_q, line - 1, line)
    pass_o(1, 2)
    qbuf[...] = (project((0,)) * scale[...] * (1.0 / math.sqrt(HD))).astype(jnp.bfloat16)

    @pl.when(c > 0)
    def _():
        kv_copy(c).wait_recv()

    q_rows = min(128, seg)
    mine = pl.ds(pl.multiple_of(t * HD, HD), HD)

    def attend(i, carry):
        rows = pl.ds(pl.multiple_of(i * q_rows, q_rows), q_rows)
        q = qbuf[rows, :]
        nt = (((1,), (1,)), ((), ()))
        s_mem = lax.dot_general(q, mem[0], nt, preferred_element_type=jnp.float32)
        s_own = lax.dot_general(q, kv[0], nt, preferred_element_type=jnp.float32)
        s_mem = jnp.where(c > 0, s_mem, -1e30)
        row = lax.broadcasted_iota(jnp.int32, s_own.shape, 0) + i * q_rows
        col = lax.broadcasted_iota(jnp.int32, s_own.shape, 1)
        s_own = jnp.where(col <= row, s_own, -1e30)
        top = jnp.maximum(
            jnp.max(s_mem, axis=1, keepdims=True), jnp.max(s_own, axis=1, keepdims=True)
        )
        e_mem = jnp.exp(s_mem - top)
        e_own = jnp.exp(s_own - top)
        total = jnp.sum(e_mem, axis=1, keepdims=True) + jnp.sum(e_own, axis=1, keepdims=True)
        mixed = jnp.dot(e_mem.astype(jnp.bfloat16), mem[1], preferred_element_type=jnp.float32)
        mixed += jnp.dot(e_own.astype(jnp.bfloat16), kv[1], preferred_element_type=jnp.float32)
        att[rows, mine] = (mixed / total).astype(jnp.bfloat16)
        return carry

    a_rows = seg // ATT_CHUNKS

    def att_copy(head, dest, i):
        part = att.at[pl.ds(i * a_rows, a_rows), pl.ds(pl.multiple_of(head * HD, HD), HD)]
        return remote(part, part, a_send.at[dest, i], a_recv.at[head, i], tp=dest)

    for i in range(ATT_CHUNKS):
        blocks = a_rows // q_rows
        lax.fori_loop(i * blocks, (i + 1) * blocks, attend, 0)
        for p in range(n_tp):
            @pl.when(p != t)
            def _():
                att_copy(t, p, i).start()

        steps = line - 2
        pass_o(2 + steps * i // ATT_CHUNKS, 2 + steps * (i + 1) // ATT_CHUNKS)

    o_forward(line - 1)
    for i in range(ATT_CHUNKS):
        for p in range(n_tp):
            @pl.when(p != t)
            def _():
                att_copy(p, p, i).wait_recv()
    for p in range(n_tp):
        part = wouse.at[1 - b, pl.ds(p * HD, HD), :]
        remote(part, part, ox_send.at[p], ox_recv.at[p], ctx=pair_c).wait_recv()

    wide = o_ref.shape[2]
    o_rows = min(128, seg)

    def final(i, carry):
        rows = pl.ds(pl.multiple_of(i * o_rows, o_rows), o_rows)
        for r in range(PAIR):
            cols = pl.ds(r * wide, wide)
            branch = jnp.dot(att[rows, :], wouse[r], preferred_element_type=jnp.float32)
            ostage[rows, cols] = (hbuf[t, rows, cols].astype(jnp.float32) + branch).astype(
                out_ref.dtype
            )
        pltpu.make_async_copy(ostage.at[rows, :], out_ref.at[rows, :], out_sem.at[i]).start()
        return carry

    lax.fori_loop(0, seg // o_rows, final, 0)

    for i in range(HIDDEN_CHUNKS):
        h_copy(t, i, hs_send.at[i], sib).wait_send()
        for q in range(n_y):
            @pl.when(q != y)
            def _():
                h_copy(t, i, hy_send.at[q, i], 2 * q + core).wait_send()
                h_copy(2 * q + core, i, hf_send.at[q, i], sib).wait_send()

    def drain(pc, carry):
        pa, parity = lax.div(pc, PAIR), lax.rem(pc, PAIR)
        right = has_right & (pa <= a)
        left = has_left & (pa >= a)
        same = parity == b

        @pl.when(right)
        def _():
            w_copy(kind_q, pc, 0).wait_send()

        @pl.when(left)
        def _():
            w_copy(kind_q, pc, 1).wait_send()

        @pl.when(same)
        def _():
            w_copy(kind_k, pc, 2).wait_send()
            w_copy(kind_v, pc, 2).wait_send()

            @pl.when(right)
            def _():
                w_copy(kind_k, pc, 0).wait_send()
                w_copy(kind_v, pc, 0).wait_send()
                o_line(pa, 0).wait_send()

            @pl.when(left)
            def _():
                w_copy(kind_k, pc, 1).wait_send()
                w_copy(kind_v, pc, 1).wait_send()
                o_line(pa, 1).wait_send()

            @pl.when(pa != t)
            def _():
                o_tp(pa).wait_send()

        return carry

    lax.fori_loop(0, n_ctx, drain, 0)
    w_copy(kind_q, c, 2).wait_send()
    for p in range(n_tp):
        o_pair(p).wait_send()

        @pl.when(p != t)
        def _():
            for i in range(ATT_CHUNKS):
                att_copy(t, p, i).wait_send()

    @pl.when(c + 1 < n_ctx)
    def _():
        kv_copy(c + 1).wait_send()

    for i in range(seg // o_rows):
        rows = pl.ds(i * o_rows, o_rows)
        pltpu.make_async_copy(ostage.at[rows, :], out_ref.at[rows, :], out_sem.at[i]).wait()


def per_device(n_ctx, n_tp, hidden, norm_gain, w_qkv, w_out):
    seg, own_d = hidden.shape
    _, kinds, depth, head = w_qkv.shape
    wide = w_out.shape[2]
    line, n_y = n_ctx // PAIR, n_tp // 2
    bf16, f32 = jnp.bfloat16, jnp.float32
    dma = pltpu.SemaphoreType.DMA
    hbm = pl.BlockSpec(memory_space=pl.ANY)
    flops = 2 * seg * own_d * n_tp * 3 * HD + 8 * seg * seg * HD + 2 * seg * HD * n_tp * own_d
    return pl.pallas_call(
        functools.partial(kernel, n_ctx, n_tp),
        out_shape=jax.ShapeDtypeStruct((seg, own_d), hidden.dtype),
        in_specs=[hbm] * 4,
        out_specs=hbm,
        scratch_shapes=[
            pltpu.VMEM((kinds, depth, head), bf16),
            pltpu.VMEM(norm_gain.shape, bf16),
            pltpu.VMEM((seg, own_d), bf16),
            pltpu.VMEM((n_tp, seg, own_d), bf16),
            pltpu.VMEM((kinds, n_ctx, depth, head), bf16),
            pltpu.VMEM((line, head, wide), bf16),
            pltpu.VMEM((PAIR, n_tp * head, wide), bf16),
            pltpu.VMEM((2, seg, head), bf16),
            pltpu.VMEM((2, seg, head), bf16),
            pltpu.VMEM((seg, head), bf16),
            pltpu.VMEM((seg, n_tp * head), bf16),
            pltpu.VMEM((seg, head), f32),
            dma((kinds, n_ctx)),
            dma((kinds, n_ctx, 3)),
            dma((line,)),
            dma((line, 2)),
            dma((n_tp,)),
            dma((line,)),
            dma((n_tp,)),
            dma((n_tp,)),
            dma((n_tp, HIDDEN_CHUNKS)),
            dma((HIDDEN_CHUNKS,)),
            dma((n_y, HIDDEN_CHUNKS)),
            dma((n_y, HIDDEN_CHUNKS)),
            dma,
            dma,
            dma((n_tp, ATT_CHUNKS)),
            dma((n_tp, ATT_CHUNKS)),
            dma((4,)),
            dma((seg // min(128, seg),)),
        ],
        compiler_params=pltpu.CompilerParams(
            collective_id=0, has_side_effects=True, vmem_limit_bytes=56 * 1024 * 1024
        ),
        cost_estimate=pl.CostEstimate(
            flops=flops, bytes_accessed=4 * seg * own_d, transcendentals=2 * seg * seg
        ),
    )(hidden, norm_gain, w_qkv, w_out)


def solution(mesh):
    n_ctx, n_tp = mesh.shape["ctx"], mesh.shape["tp"]
    placed = (P("ctx", "tp"), P(None, "ctx"), P(None, None, "ctx", "tp"), P(None, "tp", "ctx"))
    return jax.shard_map(
        functools.partial(per_device, n_ctx, n_tp),
        mesh=mesh, in_specs=placed, out_specs=P("ctx", "tp"), check_vma=False,
    )
```

```python
import functools
import math

import jax
import jax.numpy as jnp
from jax import lax
from jax.experimental import pallas as pl
from jax.experimental.pallas import tpu as pltpu
from jax.sharding import PartitionSpec as P

HD = 128
PAIR = 2
HIDDEN_CHUNKS = 2
ATT_CHUNKS = 2
KINDS = (1, 2, 0)


def kernel(
    n_ctx, n_tp,
    hid_ref, gain_ref, w_ref, o_ref, out_ref,
    wstage, gstage, ostage, hbuf, wbuf, obuf, wouse, kv, mem, qbuf, att, scale,
    w_recv, w_send, ol_recv, ol_send, ot_recv, ot_send, ox_recv, ox_send,
    h_recv, hs_send, hy_send, hf_send, kv_recv, kv_send, a_recv, a_send, in_sem, out_sem,
):
    line = n_ctx // PAIR
    n_y = n_tp // 2
    c = lax.axis_index("ctx")
    t = lax.axis_index("tp")
    a = lax.div(c, PAIR)
    b = lax.rem(c, PAIR)
    y = lax.div(t, 2)
    core = lax.rem(t, 2)
    seg, own_d = hid_ref.shape
    depth = w_ref.shape[2]
    rows_c = seg // HIDDEN_CHUNKS
    pair_c = PAIR * a + (1 - b)
    sib = 2 * y + (1 - core)
    has_right = a + 1 < line
    has_left = a >= 1

    def remote(src, dst, send, recv, ctx=None, tp=None):
        where = {}
        if ctx is not None:
            where["ctx"] = ctx
        if tp is not None:
            where["tp"] = tp
        return pltpu.make_async_remote_copy(
            src_ref=src, dst_ref=dst, send_sem=send, recv_sem=recv,
            device_id=where, device_id_type=pl.DeviceIdType.MESH,
        )

    loads = [
        pltpu.make_async_copy(gain_ref, gstage, in_sem.at[0]),
        pltpu.make_async_copy(w_ref.at[0], wstage, in_sem.at[1]),
        pltpu.make_async_copy(hid_ref, hbuf.at[t], in_sem.at[2]),
        pltpu.make_async_copy(o_ref.at[0], obuf.at[a], in_sem.at[3]),
    ]
    for load in loads:
        load.start()

    barrier = pltpu.get_barrier_semaphore()

    def greet(**where):
        pl.semaphore_signal(barrier, inc=1, device_id=where, device_id_type=pl.DeviceIdType.MESH)

    greet(ctx=pair_c)
    for p in range(n_tp):
        @pl.when(p != t)
        def _():
            greet(tp=p)

    @pl.when(has_right)
    def _():
        greet(ctx=c + PAIR)

    @pl.when(has_left)
    def _():
        greet(ctx=c - PAIR)

    @pl.when((b == 1) & (c + 1 < n_ctx))
    def _():
        greet(ctx=c + 1)

    @pl.when((b == 0) & (c > 0))
    def _():
        greet(ctx=c - 1)

    loads[0].wait()
    loads[1].wait()
    gain = jnp.transpose(jnp.broadcast_to(gstage[...].astype(jnp.float32), (HD, depth)))
    for kind in KINDS:
        wbuf[kind, c] = (wstage[kind].astype(jnp.float32) * gain).astype(jnp.bfloat16)
    loads[2].wait()
    loads[3].wait()

    @pl.when(c == 0)
    def _():
        mem[...] = jnp.zeros_like(mem)

    total = n_tp + has_right.astype(jnp.int32) + has_left.astype(jnp.int32)
    total += ((b == 1) & (c + 1 < n_ctx)).astype(jnp.int32)
    total += ((b == 0) & (c > 0)).astype(jnp.int32)
    pl.semaphore_wait(barrier, total)

    def h_part(slot, i):
        return hbuf.at[slot, pl.ds(i * rows_c, rows_c), :]

    def h_copy(slot, i, send, dest):
        part = h_part(slot, i)
        return remote(part, part, send, h_recv.at[slot, i], tp=dest)

    for i in range(HIDDEN_CHUNKS):
        for q in range(n_y):
            @pl.when(q != y)
            def _():
                h_copy(t, i, hy_send.at[q, i], 2 * q + core).start()

    def w_copy(kind, pc, way):
        slot = wbuf.at[kind, pc]
        dest = (c + PAIR, c - PAIR, pair_c)[way]
        return remote(slot, slot, w_send.at[kind, pc, way], w_recv.at[kind, pc], ctx=dest)

    def o_line(pa, way):
        slot = obuf.at[pa]
        dest = (c + PAIR, c - PAIR)[way]
        return remote(slot, slot, ol_send.at[pa, way], ol_recv.at[pa], ctx=dest)

    def o_tp(pa):
        dst = wouse.at[b, pl.ds(pl.multiple_of(t * HD, HD), HD), :]
        return remote(obuf.at[pa], dst, ot_send.at[pa], ot_recv.at[t], tp=pa)

    def o_pair(head):
        part = wouse.at[b, pl.ds(pl.multiple_of(head * HD, HD), HD), :]
        return remote(part, part, ox_send.at[head], ox_recv.at[head], ctx=pair_c)

    def line_sends(kind, pc):
        @pl.when(has_right)
        def _():
            w_copy(kind, pc, 0).start()

        @pl.when(has_left)
        def _():
            w_copy(kind, pc, 1).start()

    def own_o():
        @pl.when(has_right)
        def _():
            o_line(a, 0).start()

        @pl.when(has_left)
        def _():
            o_line(a, 1).start()

        o_route(a)

    def o_route(pa):
        @pl.when(pa == t)
        def _():
            wouse[b, pl.ds(pl.multiple_of(t * HD, HD), HD), :] = obuf[pa]
            o_pair(t).start()

        @pl.when(pa != t)
        def _():
            o_tp(pa).start()

    def w_wait(kind, pc):
        w_copy(kind, pc, 2).wait_recv()

    def pass_on(kind, first, last):
        both = kind == KINDS[-1]
        parities = (b, 1 - b) if both else (b,)

        def body(d, carry):
            for parity in parities:
                @pl.when(a - d >= 0)
                def _():
                    pc = PAIR * (a - d) + parity
                    w_wait(kind, pc)

                    @pl.when(has_right)
                    def _():
                        w_copy(kind, pc, 0).start()

                    if not both:
                        w_copy(kind, pc, 2).start()

                @pl.when(a + d < line)
                def _():
                    pc = PAIR * (a + d) + parity
                    w_wait(kind, pc)

                    @pl.when(has_left)
                    def _():
                        w_copy(kind, pc, 1).start()

                    if not both:
                        w_copy(kind, pc, 2).start()

            return carry

        lax.fori_loop(first, last, body, 0)

    def o_forward(d):
        @pl.when((a - t == d) | (t - a == d))
        def _():
            def one(p, carry):
                @pl.when(p != t)
                def _():
                    part = wouse.at[b, pl.ds(pl.multiple_of(p * HD, HD), HD), :]
                    remote(part, part, ot_send.at[0], ot_recv.at[p], tp=p).wait_recv()
                    o_pair(p).start()

                return carry

            lax.fori_loop(0, n_tp, one, 0)

    def pass_o(first, last):
        def body(d, carry):
            @pl.when(a - d >= 0)
            def _():
                o_line(a - d, 0).wait_recv()

                @pl.when(has_right)
                def _():
                    o_line(a - d, 0).start()

                o_route(a - d)

            @pl.when(a + d < line)
            def _():
                o_line(a + d, 1).wait_recv()

                @pl.when(has_left)
                def _():
                    o_line(a + d, 1).start()

                o_route(a + d)

            @pl.when(d > 1)
            def _():
                o_forward(d - 1)

            return carry

        lax.fori_loop(first, last, body, 0)

    def h_forward(i):
        for q in range(n_y):
            @pl.when(q != y)
            def _():
                slot = 2 * q + core
                h_copy(slot, i, hf_send.at[q, i], sib).wait_recv()
                h_copy(slot, i, hf_send.at[q, i], sib).start()

    def pair_wait(kind):
        def body(pa, carry):
            w_wait(kind, PAIR * pa + (1 - b))
            return carry

        lax.fori_loop(0, line, body, 0)

    kind_k, kind_v, kind_q = KINDS
    line_sends(kind_k, c)
    w_copy(kind_k, c, 2).start()
    for i in range(HIDDEN_CHUNKS):
        h_copy(t, i, hs_send.at[i], sib).start()
    line_sends(kind_v, c)
    w_copy(kind_v, c, 2).start()
    pass_on(kind_k, 1, line)
    w_copy(kind_q, c, 2).start()
    line_sends(kind_q, c)
    pass_on(kind_v, 1, line)
    w_wait(kind_q, pair_c)
    line_sends(kind_q, pair_c)
    own_o()
    pass_on(kind_q, 1, 2)
    o_forward(0)
    for i in range(HIDDEN_CHUNKS):
        h_forward(i)

    for i in range(HIDDEN_CHUNKS):
        h_copy(sib, i, hs_send.at[i], sib).wait_recv()
        for q in range(n_y):
            @pl.when(q != y)
            def _():
                h_copy(2 * q + 1 - core, i, hs_send.at[i], sib).wait_recv()

    def squares(p, sums):
        part = hbuf[p].astype(jnp.float32)
        return sums + jnp.sum(part * part, axis=1, keepdims=True)

    sums = lax.fori_loop(0, n_tp, squares, jnp.zeros((seg, 1), jnp.float32))
    scale[...] = jnp.broadcast_to(
        lax.rsqrt(sums / (own_d * n_tp) + 1e-06), scale.shape
    )

    def project(kinds):
        width = HD * len(kinds)

        def body(p, acc):
            w = [
                wbuf[k, pl.ds(PAIR * p, PAIR)].reshape(PAIR * depth, HD) for k in kinds
            ]
            w = w[0] if len(w) == 1 else jnp.concatenate(w, axis=1)
            return acc + jnp.dot(hbuf[p], w, preferred_element_type=jnp.float32)

        return lax.fori_loop(0, n_tp, body, jnp.zeros((seg, width), jnp.float32))

    pass_on(kind_q, 2, line - 1)
    pair_wait(1)
    pair_wait(2)
    proj = project((1, 2))
    kv[0] = (proj[:, :HD] * scale[...]).astype(jnp.bfloat16)
    kv[1] = (proj[:, HD:] * scale[...]).astype(jnp.bfloat16)

    def kv_copy(dest):
        return remote(kv, mem, kv_send, kv_recv, ctx=dest)

    @pl.when(c + 1 < n_ctx)
    def _():
        kv_copy(c + 1).start()

    pass_on(kind_q, line - 1, line)
    pass_o(1, 2)
    qbuf[...] = (project((0,)) * scale[...] * (1.0 / math.sqrt(HD))).astype(jnp.bfloat16)
    pass_o(2, line - 1)

    @pl.when(c > 0)
    def _():
        kv_copy(c).wait_recv()

    q_rows = min(128, seg)
    mine = pl.ds(pl.multiple_of(t * HD, HD), HD)

    def attend(i, carry):
        rows = pl.ds(pl.multiple_of(i * q_rows, q_rows), q_rows)
        q = qbuf[rows, :]
        nt = (((1,), (1,)), ((), ()))
        s_mem = lax.dot_general(q, mem[0], nt, preferred_element_type=jnp.float32)
        s_own = lax.dot_general(q, kv[0], nt, preferred_element_type=jnp.float32)
        s_mem = jnp.where(c > 0, s_mem, -1e30)
        row = lax.broadcasted_iota(jnp.int32, s_own.shape, 0) + i * q_rows
        col = lax.broadcasted_iota(jnp.int32, s_own.shape, 1)
        s_own = jnp.where(col <= row, s_own, -1e30)
        top = jnp.maximum(
            jnp.max(s_mem, axis=1, keepdims=True), jnp.max(s_own, axis=1, keepdims=True)
        )
        e_mem = jnp.exp(s_mem - top)
        e_own = jnp.exp(s_own - top)
        total = jnp.sum(e_mem, axis=1, keepdims=True) + jnp.sum(e_own, axis=1, keepdims=True)
        mixed = jnp.dot(e_mem.astype(jnp.bfloat16), mem[1], preferred_element_type=jnp.float32)
        mixed += jnp.dot(e_own.astype(jnp.bfloat16), kv[1], preferred_element_type=jnp.float32)
        att[rows, mine] = (mixed / total).astype(jnp.bfloat16)
        return carry

    a_rows = seg // ATT_CHUNKS

    def att_copy(head, dest, i):
        part = att.at[pl.ds(i * a_rows, a_rows), pl.ds(pl.multiple_of(head * HD, HD), HD)]
        return remote(part, part, a_send.at[dest, i], a_recv.at[head, i], tp=dest)

    for i in range(ATT_CHUNKS):
        blocks = a_rows // q_rows
        lax.fori_loop(i * blocks, (i + 1) * blocks, attend, 0)
        for p in range(n_tp):
            @pl.when(p != t)
            def _():
                att_copy(t, p, i).start()

    pass_o(line - 1, line)
    o_forward(line - 1)
    for i in range(ATT_CHUNKS):
        for p in range(n_tp):
            @pl.when(p != t)
            def _():
                att_copy(p, p, i).wait_recv()
    for p in range(n_tp):
        part = wouse.at[1 - b, pl.ds(p * HD, HD), :]
        remote(part, part, ox_send.at[p], ox_recv.at[p], ctx=pair_c).wait_recv()

    wide = o_ref.shape[2]
    o_rows = min(128, seg)

    def final(i, carry):
        rows = pl.ds(pl.multiple_of(i * o_rows, o_rows), o_rows)
        for r in range(PAIR):
            cols = pl.ds(r * wide, wide)
            branch = jnp.dot(att[rows, :], wouse[r], preferred_element_type=jnp.float32)
            ostage[rows, cols] = (hbuf[t, rows, cols].astype(jnp.float32) + branch).astype(
                out_ref.dtype
            )
        pltpu.make_async_copy(ostage.at[rows, :], out_ref.at[rows, :], out_sem.at[i]).start()
        return carry

    lax.fori_loop(0, seg // o_rows, final, 0)

    for i in range(HIDDEN_CHUNKS):
        h_copy(t, i, hs_send.at[i], sib).wait_send()
        for q in range(n_y):
            @pl.when(q != y)
            def _():
                h_copy(t, i, hy_send.at[q, i], 2 * q + core).wait_send()
                h_copy(2 * q + core, i, hf_send.at[q, i], sib).wait_send()

    def drain(pc, carry):
        pa, parity = lax.div(pc, PAIR), lax.rem(pc, PAIR)
        right = has_right & (pa <= a)
        left = has_left & (pa >= a)
        same = parity == b

        @pl.when(right)
        def _():
            w_copy(kind_q, pc, 0).wait_send()

        @pl.when(left)
        def _():
            w_copy(kind_q, pc, 1).wait_send()

        @pl.when(same)
        def _():
            w_copy(kind_k, pc, 2).wait_send()
            w_copy(kind_v, pc, 2).wait_send()

            @pl.when(right)
            def _():
                w_copy(kind_k, pc, 0).wait_send()
                w_copy(kind_v, pc, 0).wait_send()
                o_line(pa, 0).wait_send()

            @pl.when(left)
            def _():
                w_copy(kind_k, pc, 1).wait_send()
                w_copy(kind_v, pc, 1).wait_send()
                o_line(pa, 1).wait_send()

            @pl.when(pa != t)
            def _():
                o_tp(pa).wait_send()

        return carry

    lax.fori_loop(0, n_ctx, drain, 0)
    w_copy(kind_q, c, 2).wait_send()
    for p in range(n_tp):
        o_pair(p).wait_send()

        @pl.when(p != t)
        def _():
            for i in range(ATT_CHUNKS):
                att_copy(t, p, i).wait_send()

    @pl.when(c + 1 < n_ctx)
    def _():
        kv_copy(c + 1).wait_send()

    for i in range(seg // o_rows):
        rows = pl.ds(i * o_rows, o_rows)
        pltpu.make_async_copy(ostage.at[rows, :], out_ref.at[rows, :], out_sem.at[i]).wait()


def per_device(n_ctx, n_tp, hidden, norm_gain, w_qkv, w_out):
    seg, own_d = hidden.shape
    _, kinds, depth, head = w_qkv.shape
    wide = w_out.shape[2]
    line, n_y = n_ctx // PAIR, n_tp // 2
    bf16, f32 = jnp.bfloat16, jnp.float32
    dma = pltpu.SemaphoreType.DMA
    hbm = pl.BlockSpec(memory_space=pl.ANY)
    flops = 2 * seg * own_d * n_tp * 3 * HD + 8 * seg * seg * HD + 2 * seg * HD * n_tp * own_d
    return pl.pallas_call(
        functools.partial(kernel, n_ctx, n_tp),
        out_shape=jax.ShapeDtypeStruct((seg, own_d), hidden.dtype),
        in_specs=[hbm] * 4,
        out_specs=hbm,
        scratch_shapes=[
            pltpu.VMEM((kinds, depth, head), bf16),
            pltpu.VMEM(norm_gain.shape, bf16),
            pltpu.VMEM((seg, own_d), bf16),
            pltpu.VMEM((n_tp, seg, own_d), bf16),
            pltpu.VMEM((kinds, n_ctx, depth, head), bf16),
            pltpu.VMEM((line, head, wide), bf16),
            pltpu.VMEM((PAIR, n_tp * head, wide), bf16),
            pltpu.VMEM((2, seg, head), bf16),
            pltpu.VMEM((2, seg, head), bf16),
            pltpu.VMEM((seg, head), bf16),
            pltpu.VMEM((seg, n_tp * head), bf16),
            pltpu.VMEM((seg, head), f32),
            dma((kinds, n_ctx)),
            dma((kinds, n_ctx, 3)),
            dma((line,)),
            dma((line, 2)),
            dma((n_tp,)),
            dma((line,)),
            dma((n_tp,)),
            dma((n_tp,)),
            dma((n_tp, HIDDEN_CHUNKS)),
            dma((HIDDEN_CHUNKS,)),
            dma((n_y, HIDDEN_CHUNKS)),
            dma((n_y, HIDDEN_CHUNKS)),
            dma,
            dma,
            dma((n_tp, ATT_CHUNKS)),
            dma((n_tp, ATT_CHUNKS)),
            dma((4,)),
            dma((seg // min(128, seg),)),
        ],
        compiler_params=pltpu.CompilerParams(
            collective_id=0, has_side_effects=True, vmem_limit_bytes=56 * 1024 * 1024
        ),
        cost_estimate=pl.CostEstimate(
            flops=flops, bytes_accessed=4 * seg * own_d, transcendentals=2 * seg * seg
        ),
    )(hidden, norm_gain, w_qkv, w_out)


def solution(mesh):
    n_ctx, n_tp = mesh.shape["ctx"], mesh.shape["tp"]
    placed = (P("ctx", "tp"), P(None, "ctx"), P(None, None, "ctx", "tp"), P(None, "tp", "ctx"))
    return jax.shard_map(
        functools.partial(per_device, n_ctx, n_tp),
        mesh=mesh, in_specs=placed, out_specs=P("ctx", "tp"), check_vma=False,
    )
```

```python
import functools
import math

import jax
import jax.numpy as jnp
from jax import lax
from jax.experimental import pallas as pl
from jax.experimental.pallas import tpu as pltpu
from jax.sharding import PartitionSpec as P

HD = 128
PAIR = 2
HIDDEN_CHUNKS = 2
ATT_CHUNKS = 2
KINDS = (1, 2, 0)


def kernel(
    n_ctx, n_tp,
    hid_ref, gain_ref, w_ref, o_ref, out_ref,
    wstage, gstage, ostage, hbuf, wbuf, obuf, wouse, kv, mem, qbuf, att, scale, qacc,
    w_recv, w_send, ol_recv, ol_send, ot_recv, ot_send, ox_recv, ox_send,
    h_recv, hs_send, hy_send, hf_send, kv_recv, kv_send, a_recv, a_send, in_sem, out_sem,
):
    line = n_ctx // PAIR
    n_y = n_tp // 2
    c = lax.axis_index("ctx")
    t = lax.axis_index("tp")
    a = lax.div(c, PAIR)
    b = lax.rem(c, PAIR)
    y = lax.div(t, 2)
    core = lax.rem(t, 2)
    seg, own_d = hid_ref.shape
    depth = w_ref.shape[2]
    rows_c = seg // HIDDEN_CHUNKS
    pair_c = PAIR * a + (1 - b)
    sib = 2 * y + (1 - core)
    has_right = a + 1 < line
    has_left = a >= 1

    def remote(src, dst, send, recv, ctx=None, tp=None):
        where = {}
        if ctx is not None:
            where["ctx"] = ctx
        if tp is not None:
            where["tp"] = tp
        return pltpu.make_async_remote_copy(
            src_ref=src, dst_ref=dst, send_sem=send, recv_sem=recv,
            device_id=where, device_id_type=pl.DeviceIdType.MESH,
        )

    loads = [
        pltpu.make_async_copy(gain_ref, gstage, in_sem.at[0]),
        pltpu.make_async_copy(w_ref.at[0], wstage, in_sem.at[1]),
        pltpu.make_async_copy(hid_ref, hbuf.at[t], in_sem.at[2]),
        pltpu.make_async_copy(o_ref.at[0], obuf.at[a], in_sem.at[3]),
    ]
    for load in loads:
        load.start()

    barrier = pltpu.get_barrier_semaphore()

    def greet(**where):
        pl.semaphore_signal(barrier, inc=1, device_id=where, device_id_type=pl.DeviceIdType.MESH)

    greet(ctx=pair_c)
    for p in range(n_tp):
        @pl.when(p != t)
        def _():
            greet(tp=p)

    @pl.when(has_right)
    def _():
        greet(ctx=c + PAIR)

    @pl.when(has_left)
    def _():
        greet(ctx=c - PAIR)

    @pl.when((b == 1) & (c + 1 < n_ctx))
    def _():
        greet(ctx=c + 1)

    @pl.when((b == 0) & (c > 0))
    def _():
        greet(ctx=c - 1)

    loads[0].wait()
    loads[1].wait()
    gain = jnp.transpose(jnp.broadcast_to(gstage[...].astype(jnp.float32), (HD, depth)))
    for kind in KINDS:
        wbuf[kind, c] = (wstage[kind].astype(jnp.float32) * gain).astype(jnp.bfloat16)
    loads[2].wait()
    loads[3].wait()

    @pl.when(c == 0)
    def _():
        mem[...] = jnp.zeros_like(mem)

    total = n_tp + has_right.astype(jnp.int32) + has_left.astype(jnp.int32)
    total += ((b == 1) & (c + 1 < n_ctx)).astype(jnp.int32)
    total += ((b == 0) & (c > 0)).astype(jnp.int32)
    pl.semaphore_wait(barrier, total)

    def h_part(slot, i):
        return hbuf.at[slot, pl.ds(i * rows_c, rows_c), :]

    def h_copy(slot, i, send, dest):
        part = h_part(slot, i)
        return remote(part, part, send, h_recv.at[slot, i], tp=dest)

    for i in range(HIDDEN_CHUNKS):
        for q in range(n_y):
            @pl.when(q != y)
            def _():
                h_copy(t, i, hy_send.at[q, i], 2 * q + core).start()

    def w_copy(kind, pc, way):
        slot = wbuf.at[kind, pc]
        dest = (c + PAIR, c - PAIR, pair_c)[way]
        return remote(slot, slot, w_send.at[kind, pc, way], w_recv.at[kind, pc], ctx=dest)

    def o_line(pa, way):
        slot = obuf.at[pa]
        dest = (c + PAIR, c - PAIR)[way]
        return remote(slot, slot, ol_send.at[pa, way], ol_recv.at[pa], ctx=dest)

    def o_tp(pa):
        dst = wouse.at[b, pl.ds(pl.multiple_of(t * HD, HD), HD), :]
        return remote(obuf.at[pa], dst, ot_send.at[pa], ot_recv.at[t], tp=pa)

    def o_pair(head):
        part = wouse.at[b, pl.ds(pl.multiple_of(head * HD, HD), HD), :]
        return remote(part, part, ox_send.at[head], ox_recv.at[head], ctx=pair_c)

    def line_sends(kind, pc):
        @pl.when(has_right)
        def _():
            w_copy(kind, pc, 0).start()

        @pl.when(has_left)
        def _():
            w_copy(kind, pc, 1).start()

    def own_o():
        @pl.when(has_right)
        def _():
            o_line(a, 0).start()

        @pl.when(has_left)
        def _():
            o_line(a, 1).start()

        o_route(a)

    def o_route(pa):
        @pl.when(pa == t)
        def _():
            wouse[b, pl.ds(pl.multiple_of(t * HD, HD), HD), :] = obuf[pa]
            o_pair(t).start()

        @pl.when(pa != t)
        def _():
            o_tp(pa).start()

    def w_wait(kind, pc):
        w_copy(kind, pc, 2).wait_recv()

    def pass_on(kind, first, last):
        both = kind == KINDS[-1]
        parities = (b, 1 - b) if both else (b,)

        def body(d, carry):
            for parity in parities:
                @pl.when(a - d >= 0)
                def _():
                    pc = PAIR * (a - d) + parity
                    w_wait(kind, pc)

                    @pl.when(has_right)
                    def _():
                        w_copy(kind, pc, 0).start()

                    if not both:
                        w_copy(kind, pc, 2).start()

                @pl.when(a + d < line)
                def _():
                    pc = PAIR * (a + d) + parity
                    w_wait(kind, pc)

                    @pl.when(has_left)
                    def _():
                        w_copy(kind, pc, 1).start()

                    if not both:
                        w_copy(kind, pc, 2).start()

            return carry

        lax.fori_loop(first, last, body, 0)

    def o_forward():
        def one(p, carry):
            @pl.when(p != t)
            def _():
                part = wouse.at[b, pl.ds(pl.multiple_of(p * HD, HD), HD), :]
                remote(part, part, ot_send.at[0], ot_recv.at[p], tp=p).wait_recv()
                o_pair(p).start()

            return carry

        lax.fori_loop(0, n_tp, one, 0)

    def pass_o(first, last):
        def body(d, carry):
            @pl.when(a - d >= 0)
            def _():
                o_line(a - d, 0).wait_recv()

                @pl.when(has_right)
                def _():
                    o_line(a - d, 0).start()

                o_route(a - d)

            @pl.when(a + d < line)
            def _():
                o_line(a + d, 1).wait_recv()

                @pl.when(has_left)
                def _():
                    o_line(a + d, 1).start()

                o_route(a + d)

            return carry

        lax.fori_loop(first, last, body, 0)

    def h_forward(i):
        for q in range(n_y):
            @pl.when(q != y)
            def _():
                slot = 2 * q + core
                h_copy(slot, i, hf_send.at[q, i], sib).wait_recv()
                h_copy(slot, i, hf_send.at[q, i], sib).start()

    def pair_wait(kind):
        def body(pa, carry):
            w_wait(kind, PAIR * pa + (1 - b))
            return carry

        lax.fori_loop(0, line, body, 0)

    kind_k, kind_v, kind_q = KINDS
    w_copy(kind_q, c, 2).start()
    line_sends(kind_k, c)
    w_copy(kind_k, c, 2).start()
    for i in range(HIDDEN_CHUNKS):
        h_copy(t, i, hs_send.at[i], sib).start()
    line_sends(kind_v, c)
    w_copy(kind_v, c, 2).start()
    pass_on(kind_k, 1, line)
    own_o()
    pass_on(kind_v, 1, line)
    line_sends(kind_q, c)
    w_wait(kind_q, pair_c)
    line_sends(kind_q, pair_c)
    pass_o(1, line)
    pass_on(kind_q, 1, 2)
    for i in range(HIDDEN_CHUNKS):
        h_forward(i)

    for i in range(HIDDEN_CHUNKS):
        h_copy(sib, i, hs_send.at[i], sib).wait_recv()
        for q in range(n_y):
            @pl.when(q != y)
            def _():
                h_copy(2 * q + 1 - core, i, hs_send.at[i], sib).wait_recv()

    def squares(p, sums):
        part = hbuf[p].astype(jnp.float32)
        return sums + jnp.sum(part * part, axis=1, keepdims=True)

    sums = lax.fori_loop(0, n_tp, squares, jnp.zeros((seg, 1), jnp.float32))
    scale[...] = jnp.broadcast_to(
        lax.rsqrt(sums / (own_d * n_tp) + 1e-06), scale.shape
    )

    def project(kinds):
        width = HD * len(kinds)

        def body(p, acc):
            w = [
                wbuf[k, pl.ds(PAIR * p, PAIR)].reshape(PAIR * depth, HD) for k in kinds
            ]
            w = w[0] if len(w) == 1 else jnp.concatenate(w, axis=1)
            return acc + jnp.dot(hbuf[p], w, preferred_element_type=jnp.float32)

        return lax.fori_loop(0, n_tp, body, jnp.zeros((seg, width), jnp.float32))

    pair_wait(1)
    pair_wait(2)
    proj = project((1, 2))
    kv[0] = (proj[:, :HD] * scale[...]).astype(jnp.bfloat16)
    kv[1] = (proj[:, HD:] * scale[...]).astype(jnp.bfloat16)

    def kv_copy(dest):
        return remote(kv, mem, kv_send, kv_recv, ctx=dest)

    @pl.when(c + 1 < n_ctx)
    def _():
        kv_copy(c + 1).start()

    pass_on(kind_q, 2, line - 1)
    o_forward()

    def q_block(p):
        w = wbuf[kind_q, pl.ds(PAIR * p, PAIR)].reshape(PAIR * depth, HD)
        qacc[...] += jnp.dot(hbuf[p], w, preferred_element_type=jnp.float32)

    def q_blocks(d, carry):
        @pl.when(a - d >= 0)
        def _():
            q_block(a - d)

        @pl.when((a + d < line) & (d > 0))
        def _():
            q_block(a + d)

        return carry

    qacc[...] = jnp.zeros_like(qacc)
    lax.fori_loop(0, line - 1, q_blocks, 0)
    pass_on(kind_q, line - 1, line)
    q_blocks(line - 1, 0)
    qbuf[...] = (qacc[...] * scale[...] * (1.0 / math.sqrt(HD))).astype(jnp.bfloat16)

    @pl.when(c > 0)
    def _():
        kv_copy(c).wait_recv()

    q_rows = min(128, seg)
    mine = pl.ds(pl.multiple_of(t * HD, HD), HD)

    def attend(i, carry):
        rows = pl.ds(pl.multiple_of(i * q_rows, q_rows), q_rows)
        q = qbuf[rows, :]
        nt = (((1,), (1,)), ((), ()))
        s_mem = lax.dot_general(q, mem[0], nt, preferred_element_type=jnp.float32)
        s_own = lax.dot_general(q, kv[0], nt, preferred_element_type=jnp.float32)
        s_mem = jnp.where(c > 0, s_mem, -1e30)
        row = lax.broadcasted_iota(jnp.int32, s_own.shape, 0) + i * q_rows
        col = lax.broadcasted_iota(jnp.int32, s_own.shape, 1)
        s_own = jnp.where(col <= row, s_own, -1e30)
        top = jnp.maximum(
            jnp.max(s_mem, axis=1, keepdims=True), jnp.max(s_own, axis=1, keepdims=True)
        )
        e_mem = jnp.exp(s_mem - top)
        e_own = jnp.exp(s_own - top)
        total = jnp.sum(e_mem, axis=1, keepdims=True) + jnp.sum(e_own, axis=1, keepdims=True)
        mixed = jnp.dot(e_mem.astype(jnp.bfloat16), mem[1], preferred_element_type=jnp.float32)
        mixed += jnp.dot(e_own.astype(jnp.bfloat16), kv[1], preferred_element_type=jnp.float32)
        att[rows, mine] = (mixed / total).astype(jnp.bfloat16)
        return carry

    a_rows = seg // ATT_CHUNKS

    def att_copy(head, dest, i):
        part = att.at[pl.ds(i * a_rows, a_rows), pl.ds(pl.multiple_of(head * HD, HD), HD)]
        return remote(part, part, a_send.at[dest, i], a_recv.at[head, i], tp=dest)

    for i in range(ATT_CHUNKS):
        blocks = a_rows // q_rows
        lax.fori_loop(i * blocks, (i + 1) * blocks, attend, 0)
        for p in range(n_tp):
            @pl.when(p != t)
            def _():
                att_copy(t, p, i).start()

    for p in range(n_tp):
        part = wouse.at[1 - b, pl.ds(p * HD, HD), :]
        remote(part, part, ox_send.at[p], ox_recv.at[p], ctx=pair_c).wait_recv()

    wide = o_ref.shape[2]
    o_rows = min(128, seg)

    def final(i, carry):
        rows = pl.ds(pl.multiple_of(i * o_rows, o_rows), o_rows)
        for r in range(PAIR):
            cols = pl.ds(r * wide, wide)
            branch = jnp.dot(att[rows, :], wouse[r], preferred_element_type=jnp.float32)
            ostage[rows, cols] = (hbuf[t, rows, cols].astype(jnp.float32) + branch).astype(
                out_ref.dtype
            )
        pltpu.make_async_copy(ostage.at[rows, :], out_ref.at[rows, :], out_sem.at[i]).start()
        return carry

    for i in range(ATT_CHUNKS):
        for p in range(n_tp):
            @pl.when(p != t)
            def _():
                att_copy(p, p, i).wait_recv()
        blocks = a_rows // o_rows
        lax.fori_loop(i * blocks, (i + 1) * blocks, final, 0)

    for i in range(HIDDEN_CHUNKS):
        h_copy(t, i, hs_send.at[i], sib).wait_send()
        for q in range(n_y):
            @pl.when(q != y)
            def _():
                h_copy(t, i, hy_send.at[q, i], 2 * q + core).wait_send()
                h_copy(2 * q + core, i, hf_send.at[q, i], sib).wait_send()

    def drain(pc, carry):
        pa, parity = lax.div(pc, PAIR), lax.rem(pc, PAIR)
        right = has_right & (pa <= a)
        left = has_left & (pa >= a)
        same = parity == b

        @pl.when(right)
        def _():
            w_copy(kind_q, pc, 0).wait_send()

        @pl.when(left)
        def _():
            w_copy(kind_q, pc, 1).wait_send()

        @pl.when(same)
        def _():
            w_copy(kind_k, pc, 2).wait_send()
            w_copy(kind_v, pc, 2).wait_send()

            @pl.when(right)
            def _():
                w_copy(kind_k, pc, 0).wait_send()
                w_copy(kind_v, pc, 0).wait_send()
                o_line(pa, 0).wait_send()

            @pl.when(left)
            def _():
                w_copy(kind_k, pc, 1).wait_send()
                w_copy(kind_v, pc, 1).wait_send()
                o_line(pa, 1).wait_send()

            @pl.when(pa != t)
            def _():
                o_tp(pa).wait_send()

        return carry

    lax.fori_loop(0, n_ctx, drain, 0)
    w_copy(kind_q, c, 2).wait_send()
    for p in range(n_tp):
        o_pair(p).wait_send()

        @pl.when(p != t)
        def _():
            for i in range(ATT_CHUNKS):
                att_copy(t, p, i).wait_send()

    @pl.when(c + 1 < n_ctx)
    def _():
        kv_copy(c + 1).wait_send()

    for i in range(seg // o_rows):
        rows = pl.ds(i * o_rows, o_rows)
        pltpu.make_async_copy(ostage.at[rows, :], out_ref.at[rows, :], out_sem.at[i]).wait()


def per_device(n_ctx, n_tp, hidden, norm_gain, w_qkv, w_out):
    seg, own_d = hidden.shape
    _, kinds, depth, head = w_qkv.shape
    wide = w_out.shape[2]
    line, n_y = n_ctx // PAIR, n_tp // 2
    bf16, f32 = jnp.bfloat16, jnp.float32
    dma = pltpu.SemaphoreType.DMA
    hbm = pl.BlockSpec(memory_space=pl.ANY)
    flops = 2 * seg * own_d * n_tp * 3 * HD + 8 * seg * seg * HD + 2 * seg * HD * n_tp * own_d
    return pl.pallas_call(
        functools.partial(kernel, n_ctx, n_tp),
        out_shape=jax.ShapeDtypeStruct((seg, own_d), hidden.dtype),
        in_specs=[hbm] * 4,
        out_specs=hbm,
        scratch_shapes=[
            pltpu.VMEM((kinds, depth, head), bf16),
            pltpu.VMEM(norm_gain.shape, bf16),
            pltpu.VMEM((seg, own_d), bf16),
            pltpu.VMEM((n_tp, seg, own_d), bf16),
            pltpu.VMEM((kinds, n_ctx, depth, head), bf16),
            pltpu.VMEM((line, head, wide), bf16),
            pltpu.VMEM((PAIR, n_tp * head, wide), bf16),
            pltpu.VMEM((2, seg, head), bf16),
            pltpu.VMEM((2, seg, head), bf16),
            pltpu.VMEM((seg, head), bf16),
            pltpu.VMEM((seg, n_tp * head), bf16),
            pltpu.VMEM((seg, head), f32),
            pltpu.VMEM((seg, head), f32),
            dma((kinds, n_ctx)),
            dma((kinds, n_ctx, 3)),
            dma((line,)),
            dma((line, 2)),
            dma((n_tp,)),
            dma((line,)),
            dma((n_tp,)),
            dma((n_tp,)),
            dma((n_tp, HIDDEN_CHUNKS)),
            dma((HIDDEN_CHUNKS,)),
            dma((n_y, HIDDEN_CHUNKS)),
            dma((n_y, HIDDEN_CHUNKS)),
            dma,
            dma,
            dma((n_tp, ATT_CHUNKS)),
            dma((n_tp, ATT_CHUNKS)),
            dma((4,)),
            dma((seg // min(128, seg),)),
        ],
        compiler_params=pltpu.CompilerParams(
            collective_id=0, has_side_effects=True, vmem_limit_bytes=56 * 1024 * 1024
        ),
        cost_estimate=pl.CostEstimate(
            flops=flops, bytes_accessed=4 * seg * own_d, transcendentals=2 * seg * seg
        ),
    )(hidden, norm_gain, w_qkv, w_out)


def solution(mesh):
    n_ctx, n_tp = mesh.shape["ctx"], mesh.shape["tp"]
    placed = (P("ctx", "tp"), P(None, "ctx"), P(None, None, "ctx", "tp"), P(None, "tp", "ctx"))
    return jax.shard_map(
        functools.partial(per_device, n_ctx, n_tp),
        mesh=mesh, in_specs=placed, out_specs=P("ctx", "tp"), check_vma=False,
    )
```
